256 devices in a mesh: leaf: 32 (over x, z_hi, core), seq: 8 (over z_lo, y).
Axes of the slice: x: 4, y: 4, z: 8 (z_hi: 4, z_lo: 2; z = z_hi * 2 + z_lo), core: 2. Of those that a mesh axis runs over, the one named last changes fastest.
Arguments:
- queries: bfloat16 [32, 512, 8192], P('leaf', 'seq'), may hold values from -120 to 120
- leaf_kv: bfloat16 [32, 512, 2048], P('leaf', 'seq'), may hold values from -144 to 144
- cache: bfloat16 [4096, 2048], P(('leaf', 'seq')), may hold values from -144 to 144
- out_weight: bfloat16 [8192, 5120], P(None, 'seq'), may hold values from -0.0625 to 0.0625
- parent: int32 [48], replicated, may hold values from 0 to 15, as said below
- owner: int32 [16], replicated, may hold values from 0 to 31, as said below
- lengths: int32 [16], replicated, may hold values from 32 to 128, as said below
Outputs:
- projected: bfloat16 [32, 512, 5120], P('leaf', None, 'seq')
The draws below stay inside these ranges and needn't reach their ends.
Inputs may be any that keep to these rules, and one draw needn't show every extreme that they name: Entries 0 to 15 are segments: segment i < 4 has parent i - 1 (segment 0 has 0), the next 4 have parent 4 - 1, the next 8 each a segment of those 4; entries 16 on are the leaves, each with a parent among the last 8 segments. `owner`: distinct slots. `lengths`: some segment has exactly 128.
All inputs are finite; a program needn't handle non-finite values.
Results may differ from the reference program's by a relative error of at most 0.012.
Values may be sent and summed in bfloat16 or wider, within the bound.
No kernel may reach another device: no remote copies, remote signals or barrier semaphores. Data moves between devices by JAX's collectives and lax.ppermute only.
A program may use at most 256 MiB of HBM per device.

```python
import math
import jax
import jax.numpy as jnp
from jax import lax

D = 5120
KVH = 8
GROUP = 8
HD = 128
CAP = 128
PCH = 4
LEAF_LEN = 512
B1 = 4
B2 = 8
SEGS = 16
DEPTH = 6
N_LEAF = 32


def leaf_keys(key):
    return jnp.clip(jax.random.normal(key, (N_LEAF, LEAF_LEN, KVH, HD), jnp.float32), -6.0, 6.0)


def draw_queries(key, part):
    key = jax.random.fold_in(key, 11)
    normal_rows = jnp.clip(jax.random.normal(key, (N_LEAF, LEAF_LEN, KVH * GROUP * HD), jnp.float32), -6.0, 6.0)
    result = normal_rows
    return result.astype(jnp.bfloat16)


def draw_leaf_kv(key, part):
    base = leaf_keys(key).reshape(N_LEAF, LEAF_LEN, KVH * HD)
    key = jax.random.fold_in(key, 3)
    value_key = jax.random.fold_in(key, 1)
    keys_part = base
    values_part = 24.0 * jnp.clip(jax.random.normal(value_key, base.shape, jnp.float32), -6.0, 6.0)
    return jnp.concatenate([keys_part, values_part], axis=2).astype(jnp.bfloat16)


def draw_cache(key, part):
    key = jax.random.fold_in(key, 5)
    key_key, value_key = jax.random.split(key)
    keys_part = jnp.clip(jax.random.normal(key_key, (N_LEAF * CAP, KVH * HD), jnp.float32), -6.0, 6.0)
    values_part = 24.0 * jnp.clip(jax.random.normal(value_key, (N_LEAF * CAP, KVH * HD), jnp.float32), -6.0, 6.0)
    return jnp.concatenate([keys_part, values_part], axis=1).astype(jnp.bfloat16)


def draw_parent(key, part):
    key = jax.random.fold_in(key, 7)
    key_one, key_two, key_three, key_four = jax.random.split(key, 4)
    prompt_part = jnp.maximum(jnp.arange(PCH, dtype=jnp.int32) - 1, 0)
    first_level = jnp.full((B1,), PCH - 1, jnp.int32)
    second_pick = jnp.concatenate([jnp.arange(B1, dtype=jnp.int32), jax.random.randint(key_one, (B2 - B1,), 0, B1, jnp.int32)])
    second_level = second_pick[jax.random.permutation(key_two, B2)] + PCH
    leaf_pick = jnp.concatenate([jnp.arange(B2, dtype=jnp.int32), jax.random.randint(key_three, (N_LEAF - B2,), 0, B2, jnp.int32)])
    leaf_level = leaf_pick[jax.random.permutation(key_four, N_LEAF)] + PCH + B1
    return jnp.concatenate([prompt_part, first_level, second_level, leaf_level]).astype(jnp.int32)


def draw_owner(key, part):
    key = jax.random.fold_in(key, 13)
    return jax.random.permutation(key, N_LEAF)[:SEGS].astype(jnp.int32)


def draw_lengths(key, part):
    key = jax.random.fold_in(key, 17)
    key_one, key_two = jax.random.split(key)
    drawn = jax.random.randint(key_one, (SEGS,), CAP // 4, CAP + 1, jnp.int32)
    chosen = jax.random.randint(key_two, (), 0, SEGS, jnp.int32)
    return drawn.at[chosen].set(CAP).astype(jnp.int32)


def block_scale(own_key, dims, cuts, low, high):
    def one(axis_at, blocks):
        draws = jax.random.uniform(jax.random.fold_in(jax.random.fold_in(own_key, 6), axis_at), (blocks,), jnp.float32, low / len(cuts), high / len(cuts))
        return jnp.repeat(jnp.exp(draws), dims[axis_at] // blocks).reshape((-1,) + (1,) * (len(dims) - axis_at - 1))

    factor_of = one(*cuts[0])
    for cut in cuts[1:]:
        factor_of = factor_of * one(*cut)
    return factor_of


def noise(own_key, dims, deviation, limit, shards=(), kind=jnp.bfloat16):
    level = block_scale(own_key, dims, shards, -0.22, 0.18) if shards else 1.0
    values = jax.random.normal(own_key, dims, jnp.float32) * deviation * level
    return jnp.minimum(jnp.maximum(values, -limit), limit).astype(kind)


def setup_inputs(seed: int = 0) -> dict:
    key_list = jax.random.split(jax.random.key(seed), 8)
    queries = draw_queries(jax.random.fold_in(key_list[7], 71), 0)
    leaf_kv = draw_leaf_kv(jax.random.fold_in(key_list[7], 71), 0)
    cache = draw_cache(jax.random.fold_in(key_list[7], 71), 0)
    out_weight = noise(key_list[3], (KVH * GROUP * HD, D), (KVH * GROUP * HD) ** -0.5, 0.0625, ((1, 8),))
    parent = draw_parent(jax.random.fold_in(key_list[7], 71), 0)
    owner = draw_owner(jax.random.fold_in(key_list[7], 71), 0)
    lengths = draw_lengths(jax.random.fold_in(key_list[7], 71), 0)
    return dict(queries=queries, leaf_kv=leaf_kv, cache=cache, out_weight=out_weight, parent=parent, owner=owner, lengths=lengths)


def branch(parent, leaf_index, seg_count):
    segment = parent[seg_count + leaf_index]
    ancestry = [segment]
    for level in range(DEPTH - 1):
        segment = parent[segment]
        ancestry.append(segment)
    return jnp.stack(ancestry).astype(jnp.int32)

def reference(queries, leaf_kv, cache, out_weight, parent, owner, lengths):
    slot_cache = cache.reshape(N_LEAF, CAP, 2 * KVH * HD)
    block_rows = math.gcd(LEAF_LEN, 256)
    blocks = LEAF_LEN // block_rows
    score_scale = 1.0 / math.sqrt(HD)

    def one_leaf(leaf_index):
        ancestry = branch(parent, leaf_index, SEGS)
        branch_rows = slot_cache[owner[ancestry]].reshape(DEPTH * CAP, 2 * KVH * HD)
        branch_usable = (jnp.arange(CAP)[None, :] < lengths[ancestry][:, None]).reshape(-1)
        key_value = jnp.concatenate([branch_rows, leaf_kv[leaf_index]], axis=0).astype(jnp.float32)
        keys_all = key_value[:, :KVH * HD].reshape(-1, KVH, HD)
        values_all = key_value[:, KVH * HD:].reshape(-1, KVH, HD)
        query_rows = queries[leaf_index].reshape(blocks, block_rows, KVH, GROUP, HD)
        positions = jnp.arange(LEAF_LEN).reshape(blocks, block_rows)

        def one_block(operands):
            query_block, position = operands
            scores = jnp.einsum('qhgd,khd->qhgk', query_block.astype(jnp.float32), keys_all) * score_scale
            leaf_usable = jnp.arange(LEAF_LEN)[None, :] <= position[:, None]
            usable = jnp.concatenate([jnp.broadcast_to(branch_usable[None, :], (block_rows, DEPTH * CAP)), leaf_usable], axis=1)
            scores = jnp.where(usable[:, None, None, :], scores, -jnp.inf)
            largest = lax.optimization_barrier(jnp.max(scores, axis=3, keepdims=True))
            expon = jnp.exp(scores - largest)
            total = lax.optimization_barrier(jnp.sum(expon, axis=3))
            weights = lax.optimization_barrier(expon.astype(jnp.bfloat16))
            summed = jnp.einsum('qhgk,khd->qhgd', weights.astype(jnp.float32), values_all)
            attended = (summed / total[:, :, :, None]).astype(jnp.bfloat16)
            return attended.reshape(block_rows, KVH * GROUP * HD)
        attended = lax.map(one_block, (query_rows, positions)).reshape(LEAF_LEN, KVH * GROUP * HD)
        return jnp.dot(attended, out_weight, preferred_element_type=jnp.float32).astype(jnp.bfloat16)
    return lax.map(one_leaf, jnp.arange(N_LEAF, dtype=jnp.int32))
```

```python
import functools
import math

import jax
import jax.numpy as jnp
from jax import lax
from jax.experimental import pallas as pl
from jax.experimental.pallas import tpu as pltpu
from jax.sharding import PartitionSpec as P

KVH = 8
GROUP = 8
HD = 128
CAP = 128
DEPTH = 6
SEGS = 16
TOK = 64
UNITS = 4
QROWS = 4 * TOK
PACK = QROWS + TOK + 16
MASKED = -1e30
VMEM_LIMIT = 50 * 1024 * 1024

Z_SWAP = [(s, (s + 4) % 8) for s in range(8)]
CORE_SWAP = [(l, l ^ 1) for l in range(32)]


def y_shift(k):
    return [(z * 4 + y, z * 4 + (y + k) % 4) for z in range(2) for y in range(4)]


def x_shift(k):
    return [(l, (l + 8 * k) % 32) for l in range(32)]


def z_shift(k):
    return [
        ((x * 4 + z) * 2 + c, (x * 4 + (z + k) % 4) * 2 + c)
        for x in range(4)
        for z in range(4)
        for c in range(2)
    ]


def weight_pairs():
    pairs = []
    for x in range(4):
        for h in range(4):
            for zl in range(2):
                for y in range(4):
                    for c in range(2):
                        h_to = h if c == 0 else (h - 1 + 2 * zl) % 4
                        source = ((x * 4 + h) * 2 + c) * 8 + zl * 4 + y
                        target = ((x * 4 + h_to) * 2 + c) * 8 + (1 - zl) * 4 + y
                        pairs.append((source, target))
    return pairs


def params():
    return pltpu.CompilerParams(vmem_limit_bytes=VMEM_LIMIT)


def whole():
    return pl.BlockSpec(memory_space=pltpu.VMEM)


def anywhere():
    return pl.BlockSpec(memory_space=pl.ANY)


def scalars():
    return pl.BlockSpec(memory_space=pltpu.SMEM)


def chase(parent_ref, leaf):
    segment = parent_ref[SEGS + leaf]
    ancestry = [segment]
    for _ in range(DEPTH - 1):
        segment = parent_ref[segment]
        ancestry.append(segment)
    return ancestry


def pack_body(q_hbm, kv_hbm, cache_hbm, out_ref, q_ref, kv_ref, cache_ref, sem):
    pairs = ((kv_hbm, kv_ref), (cache_hbm, cache_ref), (q_hbm, q_ref))
    copies = [pltpu.make_async_copy(a, b, sem.at[i]) for i, (a, b) in enumerate(pairs)]
    for copy in copies:
        copy.start()
    copies[0].wait()
    copies[1].wait()
    for t in range(KVH):
        for half in range(2):
            lo = half * KVH * HD + t * HD
            cols = slice(half * HD, (half + 1) * HD)
            out_ref[t, QROWS : QROWS + TOK, cols] = kv_ref[:, lo : lo + HD]
            out_ref[t, QROWS + TOK :, cols] = cache_ref[:, lo : lo + HD]
    copies[2].wait()
    for t in range(KVH):
        for j in range(4):
            lo = t * GROUP * HD + j * 256
            out_ref[t, j * TOK : (j + 1) * TOK, :] = q_ref[:, lo : lo + 256]


def pack(queries, leaf_kv, cache):
    arrays = (queries, leaf_kv, cache)
    return pl.pallas_call(
        pack_body,
        out_shape=jax.ShapeDtypeStruct((KVH, PACK, 256), jnp.bfloat16),
        in_specs=[anywhere()] * 3,
        out_specs=whole(),
        scratch_shapes=[pltpu.VMEM(x.shape, x.dtype) for x in arrays] + [pltpu.SemaphoreType.DMA((3,))],
        compiler_params=params(),
        name="pack",
    )(*arrays)


def order_body(ids_ref, in_ref, sent_ref, first_ref, second_ref):
    step = pl.program_id(0)
    for i, out_ref in enumerate((sent_ref, first_ref, second_ref)):

        @pl.when(step // 4 == i)
        def _():
            out_ref[0] = in_ref[0, 0]


def order(ids, weight):
    cols = weight.shape[1]

    def source(i, ids):
        plane = jnp.where(i < 4, 1 - ids[2], ids[2])
        half = jnp.where(i < 8, ids[8], 1 - ids[8])
        return (plane * 4 + ids[4 + lax.rem(i, 4)], half, 0, 0)

    def target(part):
        return lambda i, ids: (jnp.clip(i - 4 * part, 0, 3), 0, 0)

    return pl.pallas_call(
        order_body,
        out_shape=[jax.ShapeDtypeStruct((4, 512, cols), jnp.bfloat16)] * 3,
        grid_spec=pltpu.PrefetchScalarGridSpec(
            num_scalar_prefetch=1,
            grid=(12,),
            in_specs=[pl.BlockSpec((1, 1, 512, cols), source)],
            out_specs=[pl.BlockSpec((1, 512, cols), target(part)) for part in range(3)],
        ),
        compiler_params=params(),
        cost_estimate=pl.CostEstimate(flops=0, bytes_accessed=24 * 512 * cols * 2, transcendentals=0),
        name="order",
    )(ids, weight.reshape(KVH, 2, 512, cols))


def join_body(units, *refs):
    outs = refs[-2:]
    for u in range(units):
        for k in range(4):
            for half in range(2):
                rows = slice(2 * TOK * u, 2 * TOK * (u + 1))
                outs[half][rows, 512 * k : 512 * (k + 1)] = refs[4 * u + k][:, 512 * half : 512 * (half + 1)]


def join(units):
    count = 2 * TOK * len(units)
    return pl.pallas_call(
        functools.partial(join_body, len(units)),
        out_shape=[jax.ShapeDtypeStruct((count, 2048), jnp.bfloat16)] * 2,
        in_specs=[whole()] * (4 * len(units)),
        out_specs=[whole()] * 2,
        compiler_params=params(),
        name="join",
    )(*[part for unit in units for part in unit])


def pick_body(flip, extra, ids_ref, parent_ref, owner_ref, *refs):
    columns = refs[:4]
    out_ref, sem = refs[-2], refs[-1]
    leaf = ids_ref[0]
    core = lax.rem(leaf, 2)
    z_hi = lax.rem(lax.div(leaf, 2), 4)
    x = lax.div(leaf, 8)
    target = leaf + flip * (1 - 2 * core)
    for act in ("start", "wait"):
        for a, segment in enumerate(chase(parent_ref, target)):
            slot = owner_ref[segment]
            here = lax.rem(slot, 2) == core
            near_x = lax.rem(x - lax.div(slot, 8) + 4, 4)
            near_z = lax.rem(z_hi - lax.rem(lax.div(slot, 2), 4) + 4, 4)
            for k in range(4):

                @pl.when(jnp.logical_and(here, near_x == k))
                def _():
                    copy = pltpu.make_async_copy(columns[k].at[near_z], out_ref.at[a], sem.at[a])
                    getattr(copy, act)()

            if extra:

                @pl.when(jnp.logical_not(here))
                def _():
                    copy = pltpu.make_async_copy(refs[4].at[a], out_ref.at[a], sem.at[a])
                    getattr(copy, act)()


def pick(flip, ids, parent, owner, columns, received=None):
    extra = received is not None
    operands = list(columns) + ([received] if extra else [])
    return pl.pallas_call(
        functools.partial(pick_body, flip, extra),
        out_shape=jax.ShapeDtypeStruct((DEPTH, CAP, 256), jnp.bfloat16),
        in_specs=[scalars()] * 3 + [anywhere()] * len(operands),
        out_specs=anywhere(),
        scratch_shapes=[pltpu.SemaphoreType.DMA((DEPTH,))],
        compiler_params=params(),
        name="pick",
    )(ids, parent, owner, *operands)


def attend_body(unit, ids_ref, parent_ref, lengths_ref, mine_ref, cache_ref, out_ref):
    first = 2 * unit
    tokens = 2 * TOK
    scale = math.log2(math.e) / math.sqrt(HD)
    limits = [lengths_ref[segment] for segment in chase(parent_ref, ids_ref[0])]
    lane = lax.broadcasted_iota(jnp.int32, (1, CAP), 1)
    bias = jnp.concatenate([jnp.where(lane < limit, 0.0, MASKED) for limit in limits], axis=1)
    cache_keys = cache_ref[:, :, :HD].reshape(DEPTH * CAP, HD)
    cache_values = cache_ref[:, :, HD:].reshape(DEPTH * CAP, HD)
    leaf_keys = mine_ref[: first + 2, QROWS : QROWS + TOK, :HD].reshape(-1, HD)
    leaf_values = mine_ref[: first + 2, QROWS : QROWS + TOK, HD:].reshape(-1, HD)
    keys = jnp.concatenate([cache_keys, leaf_keys], axis=0)
    values = jnp.concatenate([cache_values, leaf_values], axis=0)
    row = lax.broadcasted_iota(jnp.int32, (tokens, tokens), 0)
    col = lax.broadcasted_iota(jnp.int32, (tokens, tokens), 1)
    causal = jnp.where(col <= row, 0.0, MASKED)
    per = 4
    causal = jnp.concatenate([causal] * per, axis=0)
    for tile in range(GROUP // per):
        rows = []
        for g in range(tile * per, (tile + 1) * per):
            j, half = g // 2, g % 2
            part = mine_ref[first : first + 2, j * TOK : (j + 1) * TOK, half * HD : (half + 1) * HD]
            rows.append(part.reshape(tokens, HD))
        scores = lax.dot_general(
            jnp.concatenate(rows, axis=0), keys, (((1,), (1,)), ((), ())), preferred_element_type=jnp.float32
        )
        seen = DEPTH * CAP
        diagonal = seen + unit * tokens
        parts = [scores[:, :seen] + bias]
        if unit:
            parts.append(scores[:, seen:diagonal])
        parts.append(scores[:, diagonal:] + causal)
        scores = jnp.concatenate(parts, axis=1)
        largest = jnp.max(scores, axis=1, keepdims=True)
        expon = jnp.exp2((scores - largest) * scale)
        total = jnp.sum(expon, axis=1, keepdims=True)
        summed = jnp.dot(expon.astype(jnp.bfloat16), values, preferred_element_type=jnp.float32)
        done = (summed / total).astype(jnp.bfloat16)
        for i in range(per):
            g = tile * per + i
            column = pl.multiple_of(lax.rem(g + GROUP // 2 * ids_ref[8], GROUP) * HD, HD)
            out_ref[:, pl.ds(column, HD)] = done[i * tokens : (i + 1) * tokens]


def attend(unit, ids, parent, lengths, mine, cache_rows):
    keys = DEPTH * CAP + (unit + 1) * 2 * TOK
    count = 2 * TOK * GROUP
    return pl.pallas_call(
        functools.partial(attend_body, unit),
        out_shape=jax.ShapeDtypeStruct((2 * TOK, GROUP * HD), jnp.bfloat16),
        in_specs=[scalars()] * 3 + [whole()] * 2,
        out_specs=whole(),
        compiler_params=params(),
        cost_estimate=pl.CostEstimate(
            flops=count * keys * HD * 4, bytes_accessed=2_000_000, transcendentals=count * keys
        ),
        name=f"attend{unit}",
    )(ids, parent, lengths, mine, cache_rows)


def after(value, *earlier):
    return lax.optimization_barrier((value, earlier))[0]


def project(blocks, matrices):
    total = None
    for rows, matrix in zip(blocks, matrices):
        product = jnp.dot(rows, matrix.reshape(2048, -1), preferred_element_type=jnp.float32)
        total = product if total is None else total + product
    return total


def per_device(queries, leaf_kv, cache, out_weight, parent, owner, lengths):
    leaf = lax.axis_index("leaf")
    seq = lax.axis_index("seq")
    z, y, core = seq // 4, seq % 4, leaf % 2
    ids = jnp.stack([leaf, seq, z, y, y, (y + 3) % 4, (y + 1) % 4, (y + 2) % 4, core]).astype(jnp.int32)

    mine = lax.all_to_all(pack(queries[0], leaf_kv[0], cache), "seq", 0, 0)
    sent, *matrix = order(ids, out_weight)
    slot = after(mine[:, QROWS + TOK :, :].reshape(CAP, 256), sent)
    column = jnp.stack([slot] + [lax.ppermute(slot, "leaf", z_shift(k)) for k in (1, 2, 3)])
    columns = [column] + [lax.ppermute(column, "leaf", x_shift(k)) for k in (1, 2, 3)]
    near = lax.ppermute(after(sent, column), ("leaf", "seq"), weight_pairs())

    given = pick(1, ids, parent, owner, columns)
    received = lax.ppermute(given, "leaf", CORE_SWAP)
    cache_rows = pick(0, ids, parent, owner, columns, received)

    def up(part):
        return lax.ppermute(part, "seq", y_shift(1))

    def down(part):
        return lax.ppermute(part, "seq", y_shift(-1))

    def attention(unit, cache_rows):
        return attend(unit, ids, parent, lengths, mine, cache_rows)

    part0 = attention(0, cache_rows)
    up0, down0 = up(part0), down(part0)
    part1 = attention(1, after(cache_rows, part0))
    up1, down1 = up(part1), down(part1)
    part2 = attention(2, after(cache_rows, part1))
    up2, down2 = up(part2), down(part2)
    far0 = up(after(up0, part2))
    part3 = attention(3, after(cache_rows, part2, up0))
    up3, down3 = up(part3), down(part3)
    far1 = down(after(down1, part3))
    far2 = up(after(up2, part3))
    far3 = down(after(down3, part3))
    far = lax.ppermute(after(near, part3, up1, down1), "leaf", CORE_SWAP)

    low = join([(part0, up0, down0, far0), (part1, up1, down1, far1), (part2, up2, down2, far2)])
    mine_low = project(low, matrix)
    other_low = project(after(low, mine_low), (near, far)).astype(jnp.bfloat16)
    result_low = mine_low + lax.ppermute(other_low, "seq", Z_SWAP).astype(jnp.float32)
    high = join([(after(part3, other_low), up3, down3, far3)])
    other_high = project(high, (near, far)).astype(jnp.bfloat16)
    mine_high = project(after(high, other_high), matrix)
    result_high = mine_high + lax.ppermute(other_high, "seq", Z_SWAP).astype(jnp.float32)
    return jnp.concatenate([result_low, result_high], axis=0).astype(jnp.bfloat16)[None]


def solution(mesh):
    in_specs = (
        P("leaf", "seq", None),
        P("leaf", "seq", None),
        P(("leaf", "seq"), None),
        P(None, "seq"),
        P(),
        P(),
        P(),
    )
    out_specs = P("leaf", None, "seq")
    return jax.shard_map(per_device, mesh=mesh, in_specs=in_specs, out_specs=out_specs, check_vma=False)
```

```python
import functools
import math

import jax
import jax.numpy as jnp
from jax import lax
from jax.experimental import pallas as pl
from jax.experimental.pallas import tpu as pltpu
from jax.sharding import PartitionSpec as P

KVH = 8
GROUP = 8
HD = 128
CAP = 128
DEPTH = 6
SEGS = 16
TOK = 64
UNITS = 4
QROWS = 4 * TOK
MASKED = -1e30
VMEM_LIMIT = 48 * 1024 * 1024

Z_SWAP = [(s, (s + 4) % 8) for s in range(8)]
CORE_SWAP = [(l, l ^ 1) for l in range(32)]


def y_shift(k):
    return [(z * 4 + y, z * 4 + (y + k) % 4) for z in range(2) for y in range(4)]


def x_shift(k):
    return [(l, (l + 8 * k) % 32) for l in range(32)]


def z_shift(k):
    return [
        ((x * 4 + z) * 2 + c, (x * 4 + (z + k) % 4) * 2 + c)
        for x in range(4)
        for z in range(4)
        for c in range(2)
    ]


def weight_pairs(cores):
    pairs = []
    for x in range(4):
        for h in range(4):
            for zl in range(2):
                for y in range(4):
                    for c in range(2):
                        h_to = h if c in cores else (h - 1 + 2 * zl) % 4
                        source = ((x * 4 + h) * 2 + c) * 8 + zl * 4 + y
                        target = ((x * 4 + h_to) * 2 + c) * 8 + (1 - zl) * 4 + y
                        pairs.append((source, target))
    return pairs


SMALL = pl.CostEstimate(flops=1, bytes_accessed=1, transcendentals=0)


def params():
    return pltpu.CompilerParams(vmem_limit_bytes=VMEM_LIMIT)


def whole():
    return pl.BlockSpec(memory_space=pltpu.VMEM)


def anywhere():
    return pl.BlockSpec(memory_space=pl.ANY)


def scalars():
    return pl.BlockSpec(memory_space=pltpu.SMEM)


def chase(parent_ref, leaf):
    segment = parent_ref[SEGS + leaf]
    ancestry = [segment]
    for _ in range(DEPTH - 1):
        segment = parent_ref[segment]
        ancestry.append(segment)
    return ancestry


def pack_rows_body(kv_hbm, cache_hbm, *refs):
    received, (out_ref, kv_ref, cache_ref, sem) = refs[:3], refs[3:]
    copies = [
        pltpu.make_async_copy(kv_hbm.at[0], kv_ref, sem.at[0]),
        pltpu.make_async_copy(cache_hbm, cache_ref, sem.at[1]),
    ]
    for copy in copies:
        copy.start()
    for copy in copies:
        copy.wait()
    for t in range(KVH):
        for half in range(2):
            lo = half * KVH * HD + t * HD
            cols = slice(half * HD, (half + 1) * HD)
            out_ref[t, :TOK, cols] = kv_ref[:, lo : lo + HD]
            for k, slot_ref in enumerate((cache_ref, *received)):
                out_ref[t, TOK + 16 * k : TOK + 16 * (k + 1), cols] = slot_ref[:, lo : lo + HD]


def pack_rows(leaf_kv, cache, received):
    return pl.pallas_call(
        pack_rows_body,
        out_shape=jax.ShapeDtypeStruct((KVH, 2 * TOK, 256), jnp.bfloat16),
        in_specs=[pl.BlockSpec(memory_space=pltpu.HBM)] * 2 + [whole()] * 3,
        out_specs=whole(),
        scratch_shapes=[
            pltpu.VMEM(leaf_kv.shape[1:], jnp.bfloat16),
            pltpu.VMEM(cache.shape, jnp.bfloat16),
            pltpu.SemaphoreType.DMA((2,)),
        ],
        compiler_params=params(),
        cost_estimate=SMALL,
        name="pack_rows",
    )(leaf_kv, cache, *received)


def pack_queries_body(ids_ref, parent_ref, lengths_ref, q_ref, out_ref, bias_ref):
    for t in range(KVH):
        for j in range(4):
            lo = t * GROUP * HD + j * 256
            out_ref[t, j * TOK : (j + 1) * TOK, :] = q_ref[:, lo : lo + 256]
    lane = lax.broadcasted_iota(jnp.int32, (1, CAP), 1)
    for a, segment in enumerate(chase(parent_ref, ids_ref[0])):
        bias_ref[:, a * CAP : (a + 1) * CAP] = jnp.where(lane < lengths_ref[segment], 0.0, MASKED)


def pack_queries(ids, parent, lengths, queries):
    return pl.pallas_call(
        pack_queries_body,
        out_shape=[
            jax.ShapeDtypeStruct((KVH, QROWS, 256), jnp.bfloat16),
            jax.ShapeDtypeStruct((1, DEPTH * CAP), jnp.float32),
        ],
        in_specs=[scalars()] * 3 + [whole()],
        out_specs=[whole()] * 2,
        compiler_params=params(),
        cost_estimate=SMALL,
        name="pack_queries",
    )(ids, parent, lengths, queries)


def order_body(count, ids_ref, in_ref, *out_refs):
    step = pl.program_id(0)
    for i, out_ref in enumerate(out_refs):

        @pl.when(step // 4 == i)
        def _():
            out_ref[0] = in_ref[0, 0]


def order(ids, weight, here, places):
    cols = weight.shape[1]
    count = len(places)
    first, step = places[0], 1

    def source(i, ids):
        plane = ids[2] if here else 1 - ids[2]
        place = first + step * (i // 4)
        quarter = place + ids[8] * (1 - 2 * lax.rem(place, 2))
        return (plane * 4 + ids[4 + lax.rem(i, 4)], quarter, 0, 0)

    def target(part):
        return lambda i, ids: (jnp.clip(i - 4 * part, 0, 3), 0, 0)

    return pl.pallas_call(
        functools.partial(order_body, count),
        out_shape=[jax.ShapeDtypeStruct((4, 256, cols), jnp.bfloat16)] * count,
        grid_spec=pltpu.PrefetchScalarGridSpec(
            num_scalar_prefetch=1,
            grid=(4 * count,),
            in_specs=[pl.BlockSpec((1, 1, 256, cols), source)],
            out_specs=[pl.BlockSpec((1, 256, cols), target(part)) for part in range(count)],
        ),
        compiler_params=params(),
        cost_estimate=SMALL,
        name="order",
    )(ids, weight.reshape(KVH, 4, 256, cols))


def join_body(ids_ref, own_ref, up_ref, down_ref, low_ref, high_ref, *outs):
    tokens = 2 * TOK
    for place in range(4):
        quarter = place + ids_ref[8] * (1 - 2 * (place % 2))
        cols = pl.ds(pl.multiple_of(quarter * 256, 256), 256)
        for k, part_ref in enumerate((own_ref, up_ref, down_ref)):
            outs[place][:, 256 * k : 256 * (k + 1)] = part_ref[:, cols]
        outs[place][:tokens, 768:] = low_ref[:, cols]
        outs[place][tokens:, 768:] = high_ref[:, cols]


def join(ids, *parts):
    return pl.pallas_call(
        join_body,
        out_shape=[jax.ShapeDtypeStruct((4 * TOK, 1024), jnp.bfloat16)] * 4,
        in_specs=[scalars()] + [whole()] * 5,
        out_specs=[whole()] * 4,
        compiler_params=params(),
        cost_estimate=SMALL,
        name="join",
    )(ids, *parts)


def pick_body(ids_ref, parent_ref, owner_ref, *refs):
    columns, outs, sem = refs[:4], refs[4:6], refs[6]
    leaf = ids_ref[0]
    core = lax.rem(leaf, 2)
    x = lax.div(leaf, 8)
    for act in ("start", "wait"):
        for i, target in enumerate((leaf + 1 - 2 * core, leaf)):
            for a, segment in enumerate(chase(parent_ref, target)):
                slot = owner_ref[segment]
                here = lax.rem(slot, 2) == core
                near_x = lax.rem(x - lax.div(slot, 8) + 4, 4)
                near_z = lax.rem(lax.rem(lax.div(leaf, 2), 4) - lax.rem(lax.div(slot, 2), 4) + 4, 4)
                rows = pl.ds(pl.multiple_of(near_z * 16, 16), 16)
                for k in range(4):

                    @pl.when(jnp.logical_and(here, near_x == k))
                    def _():
                        copy = pltpu.make_async_copy(columns[k].at[:, rows], outs[i].at[a], sem.at[i, a])
                        getattr(copy, act)()


def pick(ids, parent, owner, columns):
    return pl.pallas_call(
        pick_body,
        out_shape=[jax.ShapeDtypeStruct((DEPTH, KVH, 16, 256), jnp.bfloat16)] * 2,
        in_specs=[scalars()] * 3 + [anywhere()] * 4,
        out_specs=[anywhere()] * 2,
        scratch_shapes=[pltpu.SemaphoreType.DMA((2, DEPTH))],
        compiler_params=params(),
        cost_estimate=SMALL,
        name="pick",
    )(ids, parent, owner, *columns)


def merge_body(ids_ref, parent_ref, owner_ref, own_ref, received_ref, out_ref, sem):
    core = lax.rem(ids_ref[0], 2)
    for act in ("start", "wait"):
        for a, segment in enumerate(chase(parent_ref, ids_ref[0])):
            here = lax.rem(owner_ref[segment], 2) == core

            @pl.when(here)
            def _():
                getattr(pltpu.make_async_copy(own_ref.at[a], out_ref.at[a], sem.at[a]), act)()

            @pl.when(jnp.logical_not(here))
            def _():
                getattr(pltpu.make_async_copy(received_ref.at[a], out_ref.at[a], sem.at[a]), act)()


def merge(ids, parent, owner, own, received):
    return pl.pallas_call(
        merge_body,
        out_shape=jax.ShapeDtypeStruct((DEPTH, KVH, 16, 256), jnp.bfloat16),
        in_specs=[scalars()] * 3 + [anywhere()] * 2,
        out_specs=anywhere(),
        scratch_shapes=[pltpu.SemaphoreType.DMA((DEPTH,))],
        compiler_params=params(),
        cost_estimate=SMALL,
        name="merge",
    )(ids, parent, owner, own, received)


def attend_body(chunk, bias_ref, mine_ref, rows_ref, cache_ref, out_ref):
    for i in range(2):
        attend_unit(2 * chunk + i, 2 * TOK * i, bias_ref, mine_ref, rows_ref, cache_ref, out_ref)


def attend_unit(unit, top, bias_ref, mine_ref, rows_ref, cache_ref, out_ref):
    first = 2 * unit
    tokens = 2 * TOK
    scale = math.log2(math.e) / math.sqrt(HD)
    bias = bias_ref[...]
    cache_keys = cache_ref[:, :, :, :HD].reshape(DEPTH * CAP, HD)
    cache_values = cache_ref[:, :, :, HD:].reshape(DEPTH * CAP, HD)
    leaf_keys = rows_ref[: first + 2, :TOK, :HD].reshape(-1, HD)
    leaf_values = rows_ref[: first + 2, :TOK, HD:].reshape(-1, HD)
    keys = jnp.concatenate([cache_keys, leaf_keys], axis=0)
    values = jnp.concatenate([cache_values, leaf_values], axis=0)
    row = lax.broadcasted_iota(jnp.int32, (tokens, tokens), 0)
    col = lax.broadcasted_iota(jnp.int32, (tokens, tokens), 1)
    causal = jnp.where(col <= row, 0.0, MASKED)
    per = 4
    causal = jnp.concatenate([causal] * per, axis=0)
    for tile in range(GROUP // per):
        rows = []
        for g in range(tile * per, (tile + 1) * per):
            j, half = g // 2, g % 2
            part = mine_ref[first : first + 2, j * TOK : (j + 1) * TOK, half * HD : (half + 1) * HD]
            rows.append(part.reshape(tokens, HD))
        scores = lax.dot_general(
            jnp.concatenate(rows, axis=0), keys, (((1,), (1,)), ((), ())), preferred_element_type=jnp.float32
        )
        seen = DEPTH * CAP
        diagonal = seen + unit * tokens
        parts = [scores[:, :seen] + bias]
        if unit:
            parts.append(scores[:, seen:diagonal])
        parts.append(scores[:, diagonal:] + causal)
        scores = jnp.concatenate(parts, axis=1)
        largest = jnp.max(scores, axis=1, keepdims=True)
        expon = jnp.exp2((scores - largest) * scale)
        total = jnp.sum(expon, axis=1, keepdims=True)
        summed = jnp.dot(expon.astype(jnp.bfloat16), values, preferred_element_type=jnp.float32)
        done = (summed / total).astype(jnp.bfloat16)
        for i in range(per):
            g = tile * per + i
            out_ref[top : top + tokens, g * HD : (g + 1) * HD] = done[i * tokens : (i + 1) * tokens]


def attend(chunk, bias, mine, rows, cache_rows):
    return pl.pallas_call(
        functools.partial(attend_body, chunk),
        out_shape=jax.ShapeDtypeStruct((4 * TOK, GROUP * HD), jnp.bfloat16),
        in_specs=[whole()] * 4,
        out_specs=whole(),
        compiler_params=params(),
        cost_estimate=pl.CostEstimate(flops=1_500_000_000, bytes_accessed=1, transcendentals=2_500_000),
        name=f"attend{chunk}",
    )(bias, mine, rows, cache_rows)


def after(value, *earlier):
    return lax.optimization_barrier((value, earlier))[0]


def project(blocks, matrices):
    total = None
    for rows, matrix in zip(blocks, matrices):
        product = jnp.dot(rows, matrix.reshape(rows.shape[1], -1), preferred_element_type=jnp.float32)
        total = product if total is None else total + product
    return total


def per_device(queries, leaf_kv, cache, out_weight, parent, owner, lengths):
    leaf = lax.axis_index("leaf")
    seq = lax.axis_index("seq")
    z, y, core = seq // 4, seq % 4, leaf % 2
    ids = jnp.stack([leaf, seq, z, y, y, (y + 3) % 4, (y + 1) % 4, (y + 2) % 4, core]).astype(jnp.int32)

    slots = [lax.ppermute(cache, "leaf", z_shift(k)) for k in (1, 2, 3)]
    (sent0,) = order(after(ids, slots[0]), out_weight, False, (0,))
    rows = lax.all_to_all(pack_rows(leaf_kv, cache, after(slots, sent0)), "seq", 0, 0)
    (sent2,) = order(after(ids, slots), out_weight, False, (2,))
    packed, bias = pack_queries(after(ids, sent2), parent, lengths, queries[0])
    column = after(rows[:, TOK:, :], packed)
    columns = [column] + [lax.ppermute(column, "leaf", x_shift(k)) for k in (1, 2, 3)]
    mine = lax.all_to_all(after(packed, rows), "seq", 0, 0)
    matrix = order(after(ids, column), out_weight, True, (0, 1, 2, 3))

    given, own = pick(after(ids, matrix), parent, owner, columns)
    received = lax.ppermute(given, "leaf", CORE_SWAP)
    cache_rows = merge(ids, parent, owner, own, received)
    near0 = lax.ppermute(after(sent0, given), ("leaf", "seq"), weight_pairs((0,)))
    near2 = lax.ppermute(after(sent2, given), ("leaf", "seq"), weight_pairs((0,)))

    def up(part):
        return lax.ppermute(part, "seq", y_shift(1))

    def down(part):
        return lax.ppermute(part, "seq", y_shift(-1))

    half = 2 * TOK
    low = attend(0, bias, mine, rows, cache_rows)
    low_up, low_down = up(low), down(low)
    high = attend(1, bias, mine, rows, after(cache_rows, low))
    high_up, high_down = up(high), down(high)
    low_far = up(after(low_up, high)[:half]), down(after(low_down, high)[half:])
    near1 = lax.ppermute(after(near0, low_up, low_down, high), "leaf", CORE_SWAP)
    near3 = lax.ppermute(after(near2, low_far, high_up, high_down), "leaf", CORE_SWAP)
    near = (near0, near1, near2, near3)
    high_far = up(after(high_up, low_far)[:half]), down(after(high_down, low_far)[half:])

    rows_low = join(ids, low, low_up, low_down, *low_far)
    other_low = project(rows_low, near).astype(jnp.bfloat16)
    mine_low = project(after(rows_low, other_low), matrix)
    other_low = lax.ppermute(other_low, "seq", Z_SWAP)
    result_low = mine_low + other_low.astype(jnp.float32)
    rows_high = join(after(ids, mine_low), high, high_up, high_down, *high_far)
    other_high = project(rows_high, near).astype(jnp.bfloat16)
    mine_high = project(after(rows_high, other_high, other_low), matrix)
    result_high = mine_high + lax.ppermute(other_high, "seq", Z_SWAP).astype(jnp.float32)
    return jnp.concatenate([result_low, result_high], axis=0).astype(jnp.bfloat16)[None]


def solution(mesh):
    in_specs = (
        P("leaf", "seq", None),
        P("leaf", "seq", None),
        P(("leaf", "seq"), None),
        P(None, "seq"),
        P(),
        P(),
        P(),
    )
    out_specs = P("leaf", None, "seq")
    return jax.shard_map(per_device, mesh=mesh, in_specs=in_specs, out_specs=out_specs, check_vma=False)
```

```python
import functools
import math

import jax
import jax.numpy as jnp
from jax import lax
from jax.experimental import pallas as pl
from jax.experimental.pallas import tpu as pltpu
from jax.sharding import PartitionSpec as P

KVH = 8
GROUP = 8
HD = 128
CAP = 128
DEPTH = 6
SEGS = 16
TOK = 64
UNITS = 4
QROWS = 4 * TOK
MASKED = -1e30
VMEM_LIMIT = 48 * 1024 * 1024

Z_SWAP = [(s, (s + 4) % 8) for s in range(8)]
CORE_SWAP = [(l, l ^ 1) for l in range(32)]


def y_shift(k):
    return [(z * 4 + y, z * 4 + (y + k) % 4) for z in range(2) for y in range(4)]


def x_shift(k):
    return [(l, (l + 8 * k) % 32) for l in range(32)]


def z_shift(k):
    return [
        ((x * 4 + z) * 2 + c, (x * 4 + (z + k) % 4) * 2 + c)
        for x in range(4)
        for z in range(4)
        for c in range(2)
    ]


def weight_pairs(cores):
    pairs = []
    for x in range(4):
        for h in range(4):
            for zl in range(2):
                for y in range(4):
                    for c in range(2):
                        h_to = h if c in cores else (h - 1 + 2 * zl) % 4
                        source = ((x * 4 + h) * 2 + c) * 8 + zl * 4 + y
                        target = ((x * 4 + h_to) * 2 + c) * 8 + (1 - zl) * 4 + y
                        pairs.append((source, target))
    return pairs


SMALL = pl.CostEstimate(flops=1, bytes_accessed=1, transcendentals=0)


def params(limit=VMEM_LIMIT):
    return pltpu.CompilerParams(vmem_limit_bytes=limit)


def whole():
    return pl.BlockSpec(memory_space=pltpu.VMEM)


def anywhere():
    return pl.BlockSpec(memory_space=pl.ANY)


def scalars():
    return pl.BlockSpec(memory_space=pltpu.SMEM)


def chase(parent_ref, leaf):
    segment = parent_ref[SEGS + leaf]
    ancestry = [segment]
    for _ in range(DEPTH - 1):
        segment = parent_ref[segment]
        ancestry.append(segment)
    return ancestry


def pack_rows_body(kv_hbm, cache_hbm, *refs):
    received, (out_ref, kv_ref, cache_ref, sem) = refs[:3], refs[3:]
    copies = [
        pltpu.make_async_copy(kv_hbm.at[0], kv_ref, sem.at[0]),
        pltpu.make_async_copy(cache_hbm, cache_ref, sem.at[1]),
    ]
    for copy in copies:
        copy.start()
    for copy in copies:
        copy.wait()
    for t in range(KVH):
        for half in range(2):
            lo = half * KVH * HD + t * HD
            cols = slice(half * HD, (half + 1) * HD)
            out_ref[t, :TOK, cols] = kv_ref[:, lo : lo + HD]
            for k, slot_ref in enumerate((cache_ref, *received)):
                out_ref[t, TOK + 16 * k : TOK + 16 * (k + 1), cols] = slot_ref[:, lo : lo + HD]


def pack_rows(leaf_kv, cache, received):
    return pl.pallas_call(
        pack_rows_body,
        out_shape=jax.ShapeDtypeStruct((KVH, 2 * TOK, 256), jnp.bfloat16),
        in_specs=[pl.BlockSpec(memory_space=pltpu.HBM)] * 2 + [whole()] * 3,
        out_specs=whole(),
        scratch_shapes=[
            pltpu.VMEM(leaf_kv.shape[1:], jnp.bfloat16),
            pltpu.VMEM(cache.shape, jnp.bfloat16),
            pltpu.SemaphoreType.DMA((2,)),
        ],
        compiler_params=params(),
        cost_estimate=SMALL,
        name="pack_rows",
    )(leaf_kv, cache, *received)


def pack_queries_body(ids_ref, parent_ref, lengths_ref, q_ref, out_ref, bias_ref):
    for t in range(KVH):
        for j in range(4):
            lo = t * GROUP * HD + j * 256
            out_ref[t, j * TOK : (j + 1) * TOK, :] = q_ref[:, lo : lo + 256]
    lane = lax.broadcasted_iota(jnp.int32, (1, CAP), 1)
    for a, segment in enumerate(chase(parent_ref, ids_ref[0])):
        bias_ref[:, a * CAP : (a + 1) * CAP] = jnp.where(lane < lengths_ref[segment], 0.0, MASKED)


def pack_queries(ids, parent, lengths, queries):
    return pl.pallas_call(
        pack_queries_body,
        out_shape=[
            jax.ShapeDtypeStruct((KVH, QROWS, 256), jnp.bfloat16),
            jax.ShapeDtypeStruct((1, DEPTH * CAP), jnp.float32),
        ],
        in_specs=[scalars()] * 3 + [whole()],
        out_specs=[whole()] * 2,
        compiler_params=params(),
        cost_estimate=SMALL,
        name="pack_queries",
    )(ids, parent, lengths, queries)


def order_body(count, ids_ref, in_ref, *out_refs):
    step = pl.program_id(0)
    for i, out_ref in enumerate(out_refs):

        @pl.when(step // 4 == i)
        def _():
            out_ref[0] = in_ref[0, 0]


def order(ids, weight, here, places):
    cols = weight.shape[1]
    count = len(places)
    first, step = places[0], 1

    def source(i, ids):
        plane = ids[2] if here else 1 - ids[2]
        place = first + step * (i // 4)
        quarter = place + ids[8] * (1 - 2 * lax.rem(place, 2))
        return (plane * 4 + ids[4 + lax.rem(i, 4)], quarter, 0, 0)

    def target(part):
        return lambda i, ids: (jnp.clip(i - 4 * part, 0, 3), 0, 0)

    return pl.pallas_call(
        functools.partial(order_body, count),
        out_shape=[jax.ShapeDtypeStruct((4, 256, cols), jnp.bfloat16)] * count,
        grid_spec=pltpu.PrefetchScalarGridSpec(
            num_scalar_prefetch=1,
            grid=(4 * count,),
            in_specs=[pl.BlockSpec((1, 1, 256, cols), source)],
            out_specs=[pl.BlockSpec((1, 256, cols), target(part)) for part in range(count)],
        ),
        compiler_params=params(),
        cost_estimate=SMALL,
        name="order",
    )(ids, weight.reshape(KVH, 4, 256, cols))


def join_body(ids_ref, own_ref, up_ref, down_ref, low_ref, high_ref, *outs):
    tokens = 2 * TOK
    for place in range(4):
        quarter = place + ids_ref[8] * (1 - 2 * (place % 2))
        cols = pl.ds(pl.multiple_of(quarter * 256, 256), 256)
        for k, part_ref in enumerate((own_ref, up_ref, down_ref)):
            outs[place][:, 256 * k : 256 * (k + 1)] = part_ref[:, cols]
        outs[place][:tokens, 768:] = low_ref[:, cols]
        outs[place][tokens:, 768:] = high_ref[:, cols]


def join(ids, *parts):
    return pl.pallas_call(
        join_body,
        out_shape=[jax.ShapeDtypeStruct((4 * TOK, 1024), jnp.bfloat16)] * 4,
        in_specs=[scalars()] + [whole()] * 5,
        out_specs=[whole()] * 4,
        compiler_params=params(VMEM_LIMIT // 3),
        cost_estimate=SMALL,
        name="join",
    )(ids, *parts)


def pick_body(ids_ref, parent_ref, owner_ref, *refs):
    columns, outs, sem = refs[:4], refs[4:6], refs[6]
    leaf = ids_ref[0]
    core = lax.rem(leaf, 2)
    x = lax.div(leaf, 8)
    for act in ("start", "wait"):
        for i, target in enumerate((leaf + 1 - 2 * core, leaf)):
            for a, segment in enumerate(chase(parent_ref, target)):
                slot = owner_ref[segment]
                here = lax.rem(slot, 2) == core
                near_x = lax.rem(x - lax.div(slot, 8) + 4, 4)
                near_z = lax.rem(lax.rem(lax.div(leaf, 2), 4) - lax.rem(lax.div(slot, 2), 4) + 4, 4)
                rows = pl.ds(pl.multiple_of(near_z * 16, 16), 16)
                for k in range(4):

                    @pl.when(jnp.logical_and(here, near_x == k))
                    def _():
                        copy = pltpu.make_async_copy(columns[k].at[:, rows], outs[i].at[a], sem.at[i, a])
                        getattr(copy, act)()


def pick(ids, parent, owner, columns):
    return pl.pallas_call(
        pick_body,
        out_shape=[jax.ShapeDtypeStruct((DEPTH, KVH, 16, 256), jnp.bfloat16)] * 2,
        in_specs=[scalars()] * 3 + [anywhere()] * 4,
        out_specs=[anywhere()] * 2,
        scratch_shapes=[pltpu.SemaphoreType.DMA((2, DEPTH))],
        compiler_params=params(),
        cost_estimate=SMALL,
        name="pick",
    )(ids, parent, owner, *columns)


def merge_body(ids_ref, parent_ref, owner_ref, own_ref, received_ref, out_ref, sem):
    core = lax.rem(ids_ref[0], 2)
    for act in ("start", "wait"):
        for a, segment in enumerate(chase(parent_ref, ids_ref[0])):
            here = lax.rem(owner_ref[segment], 2) == core

            @pl.when(here)
            def _():
                getattr(pltpu.make_async_copy(own_ref.at[a], out_ref.at[a], sem.at[a]), act)()

            @pl.when(jnp.logical_not(here))
            def _():
                getattr(pltpu.make_async_copy(received_ref.at[a], out_ref.at[a], sem.at[a]), act)()


def merge(ids, parent, owner, own, received):
    return pl.pallas_call(
        merge_body,
        out_shape=jax.ShapeDtypeStruct((DEPTH, KVH, 16, 256), jnp.bfloat16),
        in_specs=[scalars()] * 3 + [anywhere()] * 2,
        out_specs=anywhere(),
        scratch_shapes=[pltpu.SemaphoreType.DMA((DEPTH,))],
        compiler_params=params(),
        cost_estimate=SMALL,
        name="merge",
    )(ids, parent, owner, own, received)


def attend_body(chunk, bias_ref, mine_ref, rows_ref, cache_ref, out_ref):
    for i in range(2):
        attend_unit(2 * chunk + i, 2 * TOK * i, bias_ref, mine_ref, rows_ref, cache_ref, out_ref)


def attend_unit(unit, top, bias_ref, mine_ref, rows_ref, cache_ref, out_ref):
    first = 2 * unit
    tokens = 2 * TOK
    scale = math.log2(math.e) / math.sqrt(HD)
    bias = bias_ref[...]
    cache_keys = cache_ref[:, :, :, :HD].reshape(DEPTH * CAP, HD)
    cache_values = cache_ref[:, :, :, HD:].reshape(DEPTH * CAP, HD)
    leaf_keys = rows_ref[: first + 2, :TOK, :HD].reshape(-1, HD)
    leaf_values = rows_ref[: first + 2, :TOK, HD:].reshape(-1, HD)
    keys = jnp.concatenate([cache_keys, leaf_keys], axis=0)
    values = jnp.concatenate([cache_values, leaf_values], axis=0)
    row = lax.broadcasted_iota(jnp.int32, (tokens, tokens), 0)
    col = lax.broadcasted_iota(jnp.int32, (tokens, tokens), 1)
    causal = jnp.where(col <= row, 0.0, MASKED)
    per = 4
    causal = jnp.concatenate([causal] * per, axis=0)
    for tile in range(GROUP // per):
        rows = []
        for g in range(tile * per, (tile + 1) * per):
            j, half = g // 2, g % 2
            part = mine_ref[first : first + 2, j * TOK : (j + 1) * TOK, half * HD : (half + 1) * HD]
            rows.append(part.reshape(tokens, HD))
        scores = lax.dot_general(
            jnp.concatenate(rows, axis=0), keys, (((1,), (1,)), ((), ())), preferred_element_type=jnp.float32
        )
        seen = DEPTH * CAP
        diagonal = seen + unit * tokens
        parts = [scores[:, :seen] + bias]
        if unit:
            parts.append(scores[:, seen:diagonal])
        parts.append(scores[:, diagonal:] + causal)
        scores = jnp.concatenate(parts, axis=1)
        largest = jnp.max(scores, axis=1, keepdims=True)
        expon = jnp.exp2((scores - largest) * scale)
        total = jnp.sum(expon, axis=1, keepdims=True)
        summed = jnp.dot(expon.astype(jnp.bfloat16), values, preferred_element_type=jnp.float32)
        done = (summed / total).astype(jnp.bfloat16)
        for i in range(per):
            g = tile * per + i
            out_ref[top : top + tokens, g * HD : (g + 1) * HD] = done[i * tokens : (i + 1) * tokens]


def attend(chunk, bias, mine, rows, cache_rows):
    return pl.pallas_call(
        functools.partial(attend_body, chunk),
        out_shape=jax.ShapeDtypeStruct((4 * TOK, GROUP * HD), jnp.bfloat16),
        in_specs=[whole()] * 4,
        out_specs=whole(),
        compiler_params=params(VMEM_LIMIT * 2 // 3),
        cost_estimate=pl.CostEstimate(flops=1_500_000_000, bytes_accessed=1, transcendentals=2_500_000),
        name=f"attend{chunk}",
    )(bias, mine, rows, cache_rows)


def after(value, *earlier):
    return lax.optimization_barrier((value, earlier))[0]


def project(blocks, matrices):
    total = None
    for rows, matrix in zip(blocks, matrices):
        product = jnp.dot(rows, matrix.reshape(rows.shape[1], -1), preferred_element_type=jnp.float32)
        total = product if total is None else total + product
    return total


def per_device(queries, leaf_kv, cache, out_weight, parent, owner, lengths):
    leaf = lax.axis_index("leaf")
    seq = lax.axis_index("seq")
    z, y, core = seq // 4, seq % 4, leaf % 2
    ids = jnp.stack([leaf, seq, z, y, y, (y + 3) % 4, (y + 1) % 4, (y + 2) % 4, core]).astype(jnp.int32)

    slots = [lax.ppermute(cache, "leaf", z_shift(k)) for k in (1, 2, 3)]
    (sent0,) = order(after(ids, slots[0]), out_weight, False, (0,))
    rows = lax.all_to_all(pack_rows(leaf_kv, cache, after(slots, sent0)), "seq", 0, 0)
    (sent2,) = order(after(ids, slots), out_weight, False, (2,))
    packed, bias = pack_queries(after(ids, sent2), parent, lengths, queries[0])
    column = after(rows[:, TOK:, :], packed)
    columns = [column] + [lax.ppermute(column, "leaf", x_shift(k)) for k in (1, 2, 3)]
    mine = lax.all_to_all(after(packed, rows), "seq", 0, 0)
    matrix = order(after(ids, column), out_weight, True, (0, 1, 2, 3))

    given, own = pick(after(ids, matrix), parent, owner, columns)
    received = lax.ppermute(given, "leaf", CORE_SWAP)
    cache_rows = merge(ids, parent, owner, own, received)
    near0 = lax.ppermute(after(sent0, given), ("leaf", "seq"), weight_pairs((0,)))
    near2 = lax.ppermute(after(sent2, given), ("leaf", "seq"), weight_pairs((0,)))

    def up(part):
        return lax.ppermute(part, "seq", y_shift(1))

    def down(part):
        return lax.ppermute(part, "seq", y_shift(-1))

    half = 2 * TOK
    low = attend(0, bias, mine, rows, cache_rows)
    low_up, low_down = up(low), down(low)
    high = attend(1, bias, mine, rows, after(cache_rows, low))
    high_up, high_down = up(high), down(high)
    low_far = up(after(low_up, high)[:half]), down(after(low_down, high)[half:])
    near1 = lax.ppermute(after(near0, low_up, low_down, high), "leaf", CORE_SWAP)
    near3 = lax.ppermute(after(near2, low_far, high_up, high_down), "leaf", CORE_SWAP)
    near = (near0, near1, near2, near3)
    high_far = up(after(high_up, low_far)[:half]), down(after(high_down, low_far)[half:])

    rows_low = join(ids, low, low_up, low_down, *low_far)
    other_low = project(rows_low, near).astype(jnp.bfloat16)
    rows_high = join(after(ids, other_low), high, high_up, high_down, *high_far)
    other_high = project(rows_high, near).astype(jnp.bfloat16)
    other_low = lax.ppermute(other_low, "seq", Z_SWAP)
    mine_low = project(after(rows_low, other_high, other_low), matrix)
    result_low = mine_low + other_low.astype(jnp.float32)
    mine_high = project(after(rows_high, mine_low), matrix)
    result_high = mine_high + lax.ppermute(other_high, "seq", Z_SWAP).astype(jnp.float32)
    return jnp.concatenate([result_low, result_high], axis=0).astype(jnp.bfloat16)[None]


def solution(mesh):
    in_specs = (
        P("leaf", "seq", None),
        P("leaf", "seq", None),
        P(("leaf", "seq"), None),
        P(None, "seq"),
        P(),
        P(),
        P(),
    )
    out_specs = P("leaf", None, "seq")
    return jax.shard_map(per_device, mesh=mesh, in_specs=in_specs, out_specs=out_specs, check_vma=False)
```

```python
import functools
import math

import jax
import jax.numpy as jnp
from jax import lax
from jax.experimental import pallas as pl
from jax.experimental.pallas import tpu as pltpu
from jax.sharding import PartitionSpec as P

KVH = 8
GROUP = 8
HD = 128
CAP = 128
DEPTH = 6
SEGS = 16
TOK = 64
UNITS = 4
QROWS = 4 * TOK
MASKED = -1e30
VMEM_LIMIT = 48 * 1024 * 1024

Z_SWAP = [(s, (s + 4) % 8) for s in range(8)]
CORE_SWAP = [(l, l ^ 1) for l in range(32)]


def y_shift(k):
    return [(z * 4 + y, z * 4 + (y + k) % 4) for z in range(2) for y in range(4)]


def x_shift(k):
    return [(l, (l + 8 * k) % 32) for l in range(32)]


def z_shift(k):
    return [
        ((x * 4 + z) * 2 + c, (x * 4 + (z + k) % 4) * 2 + c)
        for x in range(4)
        for z in range(4)
        for c in range(2)
    ]


def weight_pairs(cores):
    pairs = []
    for x in range(4):
        for h in range(4):
            for zl in range(2):
                for y in range(4):
                    for c in range(2):
                        h_to = h if c in cores else (h - 1 + 2 * zl) % 4
                        source = ((x * 4 + h) * 2 + c) * 8 + zl * 4 + y
                        target = ((x * 4 + h_to) * 2 + c) * 8 + (1 - zl) * 4 + y
                        pairs.append((source, target))
    return pairs


SMALL = pl.CostEstimate(flops=1, bytes_accessed=1, transcendentals=0)


def params(limit=VMEM_LIMIT):
    return pltpu.CompilerParams(vmem_limit_bytes=limit)


def whole():
    return pl.BlockSpec(memory_space=pltpu.VMEM)


def anywhere():
    return pl.BlockSpec(memory_space=pl.ANY)


def scalars():
    return pl.BlockSpec(memory_space=pltpu.SMEM)


def chase(parent_ref, leaf):
    segment = parent_ref[SEGS + leaf]
    ancestry = [segment]
    for _ in range(DEPTH - 1):
        segment = parent_ref[segment]
        ancestry.append(segment)
    return ancestry


def pack_rows_body(kv_hbm, cache_hbm, *refs):
    received, (out_ref, kv_ref, cache_ref, sem) = refs[:3], refs[3:]
    copies = [
        pltpu.make_async_copy(kv_hbm.at[0], kv_ref, sem.at[0]),
        pltpu.make_async_copy(cache_hbm, cache_ref, sem.at[1]),
    ]
    for copy in copies:
        copy.start()
    for copy in copies:
        copy.wait()
    for t in range(KVH):
        for half in range(2):
            lo = half * KVH * HD + t * HD
            cols = slice(half * HD, (half + 1) * HD)
            out_ref[t, :TOK, cols] = kv_ref[:, lo : lo + HD]
            for k, slot_ref in enumerate((cache_ref, *received)):
                out_ref[t, TOK + 16 * k : TOK + 16 * (k + 1), cols] = slot_ref[:, lo : lo + HD]


def pack_rows(leaf_kv, cache, received):
    return pl.pallas_call(
        pack_rows_body,
        out_shape=jax.ShapeDtypeStruct((KVH, 2 * TOK, 256), jnp.bfloat16),
        in_specs=[pl.BlockSpec(memory_space=pltpu.HBM)] * 2 + [whole()] * 3,
        out_specs=whole(),
        scratch_shapes=[
            pltpu.VMEM(leaf_kv.shape[1:], jnp.bfloat16),
            pltpu.VMEM(cache.shape, jnp.bfloat16),
            pltpu.SemaphoreType.DMA((2,)),
        ],
        compiler_params=params(),
        cost_estimate=SMALL,
        name="pack_rows",
    )(leaf_kv, cache, *received)


def pack_queries_body(ids_ref, parent_ref, lengths_ref, q_ref, out_ref, bias_ref):
    for t in range(KVH):
        for j in range(4):
            lo = t * GROUP * HD + j * 256
            out_ref[t, j * TOK : (j + 1) * TOK, :] = q_ref[:, lo : lo + 256]
    lane = lax.broadcasted_iota(jnp.int32, (1, CAP), 1)
    for a, segment in enumerate(chase(parent_ref, ids_ref[0])):
        bias_ref[:, a * CAP : (a + 1) * CAP] = jnp.where(lane < lengths_ref[segment], 0.0, MASKED)


def pack_queries(ids, parent, lengths, queries):
    return pl.pallas_call(
        pack_queries_body,
        out_shape=[
            jax.ShapeDtypeStruct((KVH, QROWS, 256), jnp.bfloat16),
            jax.ShapeDtypeStruct((1, DEPTH * CAP), jnp.float32),
        ],
        in_specs=[scalars()] * 3 + [whole()],
        out_specs=[whole()] * 2,
        compiler_params=params(),
        cost_estimate=SMALL,
        name="pack_queries",
    )(ids, parent, lengths, queries)


def order_body(count, ids_ref, in_ref, *out_refs):
    step = pl.program_id(0)
    for i, out_ref in enumerate(out_refs):

        @pl.when(step // 4 == i)
        def _():
            out_ref[0] = in_ref[0, 0]


def order(ids, weight, here, places):
    cols = weight.shape[1]
    count = len(places)
    first, step = places[0], 1

    def source(i, ids):
        plane = ids[2] if here else 1 - ids[2]
        place = first + step * (i // 4)
        quarter = place + ids[8] * (1 - 2 * lax.rem(place, 2))
        return (plane * 4 + ids[4 + lax.rem(i, 4)], quarter, 0, 0)

    def target(part):
        return lambda i, ids: (jnp.clip(i - 4 * part, 0, 3), 0, 0)

    return pl.pallas_call(
        functools.partial(order_body, count),
        out_shape=[jax.ShapeDtypeStruct((4, 256, cols), jnp.bfloat16)] * count,
        grid_spec=pltpu.PrefetchScalarGridSpec(
            num_scalar_prefetch=1,
            grid=(4 * count,),
            in_specs=[pl.BlockSpec((1, 1, 256, cols), source)],
            out_specs=[pl.BlockSpec((1, 256, cols), target(part)) for part in range(count)],
        ),
        compiler_params=params(),
        cost_estimate=SMALL,
        name="order",
    )(ids, weight.reshape(KVH, 4, 256, cols))


def join_body(ids_ref, own_ref, up_ref, down_ref, low_ref, high_ref, *outs):
    tokens = 2 * TOK
    for place in range(4):
        quarter = place + ids_ref[8] * (1 - 2 * (place % 2))
        cols = pl.ds(pl.multiple_of(quarter * 256, 256), 256)
        for k, part_ref in enumerate((own_ref, up_ref, down_ref)):
            outs[place][:, 256 * k : 256 * (k + 1)] = part_ref[:, cols]
        outs[place][:tokens, 768:] = low_ref[:, cols]
        outs[place][tokens:, 768:] = high_ref[:, cols]


def join(ids, *parts):
    return pl.pallas_call(
        join_body,
        out_shape=[jax.ShapeDtypeStruct((4 * TOK, 1024), jnp.bfloat16)] * 4,
        in_specs=[scalars()] + [whole()] * 5,
        out_specs=[whole()] * 4,
        compiler_params=params(VMEM_LIMIT // 3),
        cost_estimate=SMALL,
        name="join",
    )(ids, *parts)


def pick_body(ids_ref, parent_ref, owner_ref, *refs):
    columns, outs, sem = refs[:4], refs[4:6], refs[6]
    leaf = ids_ref[0]
    core = lax.rem(leaf, 2)
    x = lax.div(leaf, 8)
    for act in ("start", "wait"):
        for i, target in enumerate((leaf + 1 - 2 * core, leaf)):
            for a, segment in enumerate(chase(parent_ref, target)):
                slot = owner_ref[segment]
                here = lax.rem(slot, 2) == core
                near_x = lax.rem(x - lax.div(slot, 8) + 4, 4)
                near_z = lax.rem(lax.rem(lax.div(leaf, 2), 4) - lax.rem(lax.div(slot, 2), 4) + 4, 4)
                rows = pl.ds(pl.multiple_of(near_z * 16, 16), 16)
                for k in range(4):

                    @pl.when(jnp.logical_and(here, near_x == k))
                    def _():
                        copy = pltpu.make_async_copy(columns[k].at[:, rows], outs[i].at[a], sem.at[i, a])
                        getattr(copy, act)()


def pick(ids, parent, owner, columns):
    return pl.pallas_call(
        pick_body,
        out_shape=[jax.ShapeDtypeStruct((DEPTH, KVH, 16, 256), jnp.bfloat16)] * 2,
        in_specs=[scalars()] * 3 + [anywhere()] * 4,
        out_specs=[anywhere()] * 2,
        scratch_shapes=[pltpu.SemaphoreType.DMA((2, DEPTH))],
        compiler_params=params(),
        cost_estimate=SMALL,
        name="pick",
    )(ids, parent, owner, *columns)


def merge_body(ids_ref, parent_ref, owner_ref, own_ref, received_ref, out_ref, sem):
    core = lax.rem(ids_ref[0], 2)
    for act in ("start", "wait"):
        for a, segment in enumerate(chase(parent_ref, ids_ref[0])):
            here = lax.rem(owner_ref[segment], 2) == core

            @pl.when(here)
            def _():
                getattr(pltpu.make_async_copy(own_ref.at[a], out_ref.at[a], sem.at[a]), act)()

            @pl.when(jnp.logical_not(here))
            def _():
                getattr(pltpu.make_async_copy(received_ref.at[a], out_ref.at[a], sem.at[a]), act)()


def merge(ids, parent, owner, own, received):
    return pl.pallas_call(
        merge_body,
        out_shape=jax.ShapeDtypeStruct((DEPTH, KVH, 16, 256), jnp.bfloat16),
        in_specs=[scalars()] * 3 + [anywhere()] * 2,
        out_specs=anywhere(),
        scratch_shapes=[pltpu.SemaphoreType.DMA((DEPTH,))],
        compiler_params=params(),
        cost_estimate=SMALL,
        name="merge",
    )(ids, parent, owner, own, received)


def attend_body(chunk, bias_ref, mine_ref, rows_ref, cache_ref, out_ref):
    for i in range(2):
        attend_unit(2 * chunk + i, 2 * TOK * i, bias_ref, mine_ref, rows_ref, cache_ref, out_ref)


def attend_unit(unit, top, bias_ref, mine_ref, rows_ref, cache_ref, out_ref):
    first = 2 * unit
    tokens = 2 * TOK
    scale = math.log2(math.e) / math.sqrt(HD)
    bias = bias_ref[...]
    cache_keys = cache_ref[:, :, :, :HD].reshape(DEPTH * CAP, HD)
    cache_values = cache_ref[:, :, :, HD:].reshape(DEPTH * CAP, HD)
    leaf_keys = rows_ref[: first + 2, :TOK, :HD].reshape(-1, HD)
    leaf_values = rows_ref[: first + 2, :TOK, HD:].reshape(-1, HD)
    keys = jnp.concatenate([cache_keys, leaf_keys], axis=0)
    values = jnp.concatenate([cache_values, leaf_values], axis=0)
    values = jnp.concatenate([values, jnp.ones_like(values)], axis=1)
    row = lax.broadcasted_iota(jnp.int32, (tokens, tokens), 0)
    col = lax.broadcasted_iota(jnp.int32, (tokens, tokens), 1)
    causal = jnp.where(col <= row, 0.0, MASKED)
    per = 4
    causal = jnp.concatenate([causal] * per, axis=0)
    for tile in range(GROUP // per):
        rows = []
        for g in range(tile * per, (tile + 1) * per):
            j, half = g // 2, g % 2
            part = mine_ref[first : first + 2, j * TOK : (j + 1) * TOK, half * HD : (half + 1) * HD]
            rows.append(part.reshape(tokens, HD))
        scores = lax.dot_general(
            jnp.concatenate(rows, axis=0), keys, (((1,), (1,)), ((), ())), preferred_element_type=jnp.float32
        )
        seen = DEPTH * CAP
        diagonal = seen + unit * tokens
        parts = [scores[:, :seen] + bias]
        if unit:
            parts.append(scores[:, seen:diagonal])
        parts.append(scores[:, diagonal:] + causal)
        scores = jnp.concatenate(parts, axis=1)
        largest = jnp.max(scores, axis=1, keepdims=True)
        expon = jnp.exp2((scores - largest) * scale)
        both = jnp.dot(expon.astype(jnp.bfloat16), values, preferred_element_type=jnp.float32)
        done = (both[:, :HD] / both[:, HD:]).astype(jnp.bfloat16)
        for i in range(per):
            g = tile * per + i
            out_ref[top : top + tokens, g * HD : (g + 1) * HD] = done[i * tokens : (i + 1) * tokens]


def attend(chunk, bias, mine, rows, cache_rows):
    return pl.pallas_call(
        functools.partial(attend_body, chunk),
        out_shape=jax.ShapeDtypeStruct((4 * TOK, GROUP * HD), jnp.bfloat16),
        in_specs=[whole()] * 4,
        out_specs=whole(),
        compiler_params=params(VMEM_LIMIT * 2 // 3),
        cost_estimate=pl.CostEstimate(flops=1_500_000_000, bytes_accessed=1, transcendentals=2_500_000),
        name=f"attend{chunk}",
    )(bias, mine, rows, cache_rows)


def after(value, *earlier):
    return lax.optimization_barrier((value, earlier))[0]


def project(blocks, matrices):
    total = None
    for rows, matrix in zip(blocks, matrices):
        product = jnp.dot(rows, matrix.reshape(rows.shape[1], -1), preferred_element_type=jnp.float32)
        total = product if total is None else total + product
    return total


def per_device(queries, leaf_kv, cache, out_weight, parent, owner, lengths):
    leaf = lax.axis_index("leaf")
    seq = lax.axis_index("seq")
    z, y, core = seq // 4, seq % 4, leaf % 2
    ids = jnp.stack([leaf, seq, z, y, y, (y + 3) % 4, (y + 1) % 4, (y + 2) % 4, core]).astype(jnp.int32)

    slots = [lax.ppermute(cache, "leaf", z_shift(k)) for k in (1, 2, 3)]
    (sent0,) = order(after(ids, slots[0]), out_weight, False, (0,))
    rows = lax.all_to_all(pack_rows(leaf_kv, cache, after(slots, sent0)), "seq", 0, 0)
    (sent2,) = order(after(ids, slots), out_weight, False, (2,))
    packed, bias = pack_queries(after(ids, sent2), parent, lengths, queries[0])
    column = after(rows[:, TOK:, :], packed)
    columns = [column] + [lax.ppermute(column, "leaf", x_shift(k)) for k in (1, 2, 3)]
    mine = lax.all_to_all(after(packed, rows), "seq", 0, 0)
    matrix = order(after(ids, column), out_weight, True, (0, 1, 2, 3))

    given, own = pick(after(ids, matrix), parent, owner, columns)
    received = lax.ppermute(given, "leaf", CORE_SWAP)
    cache_rows = merge(ids, parent, owner, own, received)
    near0 = lax.ppermute(after(sent0, given), ("leaf", "seq"), weight_pairs((0,)))
    near2 = lax.ppermute(after(sent2, given), ("leaf", "seq"), weight_pairs((0,)))

    def up(part):
        return lax.ppermute(part, "seq", y_shift(1))

    def down(part):
        return lax.ppermute(part, "seq", y_shift(-1))

    half = 2 * TOK
    low = attend(0, bias, mine, rows, cache_rows)
    low_up, low_down = up(low), down(low)
    high = attend(1, bias, mine, rows, after(cache_rows, low))
    high_up, high_down = up(high), down(high)
    low_far = up(after(low_up, high)[:half]), down(after(low_down, high)[half:])
    near1 = lax.ppermute(after(near0, low_up, low_down, high), "leaf", CORE_SWAP)
    near3 = lax.ppermute(after(near2, low_far, high_up, high_down), "leaf", CORE_SWAP)
    near = (near0, near1, near2, near3)
    high_far = up(after(high_up, low_far)[:half]), down(after(high_down, low_far)[half:])

    rows_low = join(ids, low, low_up, low_down, *low_far)
    other_low = project(rows_low, near).astype(jnp.bfloat16)
    rows_high = join(after(ids, other_low), high, high_up, high_down, *high_far)
    other_high = project(rows_high, near).astype(jnp.bfloat16)
    other_low = lax.ppermute(other_low, "seq", Z_SWAP)
    mine_low = project(after(rows_low, other_high, other_low), matrix)
    result_low = mine_low + other_low.astype(jnp.float32)
    mine_high = project(after(rows_high, mine_low), matrix)
    result_high = mine_high + lax.ppermute(other_high, "seq", Z_SWAP).astype(jnp.float32)
    return jnp.concatenate([result_low, result_high], axis=0).astype(jnp.bfloat16)[None]


def solution(mesh):
    in_specs = (
        P("leaf", "seq", None),
        P("leaf", "seq", None),
        P(("leaf", "seq"), None),
        P(None, "seq"),
        P(),
        P(),
        P(),
    )
    out_specs = P("leaf", None, "seq")
    return jax.shard_map(per_device, mesh=mesh, in_specs=in_specs, out_specs=out_specs, check_vma=False)
```
